32 devices in a mesh: groups: 2 (over x), row: 16 (over z, y, core).
Axes of the slice: x: 2, y: 2, z: 4, core: 2. Of those that a mesh axis runs over, the one named last changes fastest.
Arguments:
- amplitudes: float32 [6144, 16384], P('row', 'groups'), parts along dimension 1, may hold values from -6 to 6
- integrals: float32 [6144, 1024], P('row', 'groups'), parts along dimension 1, may hold values from -0.21875 to 0.21875
- pair_irrep: int32 [192], P('groups'), parts along dimension 0, may hold values from 0 to 7
- column_irrep: int32 [16], P('groups'), parts along dimension 0, may hold values from 0 to 7
Outputs:
- cycle_term: float32 [8192, 1024], P('row', 'groups'), parts along dimension 1
The draws below stay inside these ranges and needn't reach their ends.
There are 2 independent parts, one for each index of `groups`. The reference program is written for one: setup_inputs(seed, part) draws one part's arguments, and reference() takes and returns one part's arrays. A program takes and returns all parts, laid end to end along the dimension named above; each array names one. Nothing has to cross between parts.
All inputs are finite; a program needn't handle non-finite values.
Results may differ from the reference program's by a relative error of at most 0.000075.
Values sent between devices are 32-bit elements; how exact they have to be, the bound alone decides.
A program may use at most 128 MiB of HBM per device.

```python
import jax
import jax.numpy as jnp
from jax import lax

KW = 6144
NC = 512
TILE = 64
M = 8192
KT = 96
NT = 8


def set_ends(values, rng, smallest, high):
    dims = values.shape
    index_at = [jax.random.randint(jax.random.fold_in(rng, axis), (), 0, dims[axis]) for axis in range(len(dims))]
    values = values.at[tuple(index_at)].set(smallest)
    longest = dims.index(max(dims))
    index_at[longest] = (index_at[longest] + 1) % dims[longest]
    return values.at[tuple(index_at)].set(high)


def block_scale(stream_key, extent, shards, smallest, high):
    gain = 1.0
    for dim, blocks in shards:
        steps = jax.random.uniform(jax.random.fold_in(jax.random.fold_in(stream_key, 6), dim), (blocks,), jnp.float32, smallest / len(shards), high / len(shards))
        gain = gain * jnp.repeat(jnp.exp(steps), extent[dim] // blocks).reshape((-1,) + (1,) * (len(extent) - 1 - dim))
    return gain


def bell_draw(own_key, dims, width, most, split=(), dtype=jnp.bfloat16):
    values = jax.random.normal(own_key, dims, jnp.float32) * width
    if len(split) > 0:
        values = block_scale(own_key, dims, split, -0.22, 0.18) * values
    return jnp.clip(values, min=-most, max=most).astype(dtype)


def setup_inputs(seed: int = 0, part: int = 0) -> dict:
    arg_keys = jax.random.split(jax.random.key(seed), 5)
    part_splits = jax.random.split(jax.random.fold_in(arg_keys[4], part), 5)
    amplitudes = bell_draw(part_splits[0], (KW, M), 1.0, 6.0, ((0, 16),), jnp.float32)
    integrals = bell_draw(part_splits[1], (KW, NC), (KW // 8) ** -0.5, 0.21875, ((0, 16),), jnp.float32)
    pair_irrep = set_ends(jax.random.randint(part_splits[2], (KT,), 0, 8), jax.random.fold_in(part_splits[2], 1), 0, 7).astype(jnp.int32)
    column_irrep = set_ends(jax.random.randint(part_splits[3], (NT,), 0, 8), jax.random.fold_in(part_splits[3], 1), 0, 7).astype(jnp.int32)
    return dict(amplitudes=amplitudes, integrals=integrals, pair_irrep=pair_irrep, column_irrep=column_irrep)


def reference(amplitudes, integrals, pair_irrep, column_irrep):
    row_labels = jnp.broadcast_to(pair_irrep[:, None], (KT, TILE)).reshape(KW)
    col_labels = jnp.broadcast_to(column_irrep[:, None], (NT, TILE)).reshape(NC)
    allowed = row_labels[:, None] == col_labels[None, :]
    masked = jnp.where(allowed, integrals, jnp.zeros_like(integrals))
    return lax.dot_general(amplitudes, masked, (((0,), (0,)), ((), ())),
                           precision=lax.Precision.HIGHEST,
                           preferred_element_type=jnp.float32)
```

```python
import functools

import jax
import jax.numpy as jnp
from jax import lax
from jax.experimental import pallas as pl
from jax.experimental.pallas import tpu as pltpu
from jax.sharding import PartitionSpec as P

TILE = 64
MESH = pl.DeviceIdType.MESH
CHUNKS = 4


def split(x):
    high = x.astype(jnp.bfloat16)
    low = (x - high.astype(jnp.float32)).astype(jnp.bfloat16)
    return high, low


def kernel(depth, a_hbm, b_hbm, pair_ref, column_ref, out_ref, a_buf, b_buf, b_high, b_low, part, from_y, from_z,
           a_sem, b_sem, a_send, a_recv, b_send, b_recv, y_send, y_recv, z_send, z_recv):
    local_k, width = b_hbm.shape
    rows = out_ref.shape[0]
    chunk = rows // CHUNKS
    me = lax.axis_index("row")
    z, y, c = me // 4, (me // 2) % 2, me % 2
    sibling = me + 1 - 2 * c
    across = me + 2 - 4 * y
    up, down = z < depth - 1, z > 0

    order = []
    low, high = z * 0, z * 0 + depth - 1
    for _ in range(depth):
        take_high = (high - z) > (z - low)
        order.append(jnp.where(take_high, high, low))
        low, high = jnp.where(take_high, low, low + 1), jnp.where(take_high, high - 1, high)

    def layer(s):
        found = order[0]
        for k in range(1, depth):
            found = jnp.where(s == k, order[k], found)
        return found

    def columns(b, core):
        other = 1 - b // depth
        side = y + other * (1 - 2 * y)
        owner = 4 * layer(b % depth) + 2 * side + core
        return pl.ds(pl.multiple_of(owner * rows, rows), rows)

    def a_local(b):
        return pltpu.make_async_copy(a_hbm.at[:, columns(b, c)], a_buf.at[b, pl.ds(0, local_k)], a_sem.at[b])

    def a_swap(b):
        return pltpu.make_async_remote_copy(
            src_ref=a_hbm.at[:, columns(b, 1 - c)], dst_ref=a_buf.at[b, pl.ds(local_k, local_k)],
            send_sem=a_send.at[b], recv_sem=a_recv.at[b], device_id={"row": sibling}, device_id_type=MESH)

    b_local = pltpu.make_async_copy(b_hbm, b_buf.at[pl.ds(0, local_k)], b_sem)
    b_swap = pltpu.make_async_remote_copy(
        src_ref=b_hbm, dst_ref=b_buf.at[pl.ds(local_k, local_k)], send_sem=b_send, recv_sem=b_recv,
        device_id={"row": sibling}, device_id_type=MESH)

    def y_copy(s, q):
        span = pl.ds(q * chunk, chunk)
        return pltpu.make_async_remote_copy(
            src_ref=part.at[s, span], dst_ref=from_y.at[s, span], send_sem=y_send.at[s, q], recv_sem=y_recv.at[s, q],
            device_id={"row": across}, device_id_type=MESH)

    def z_copy(s, q):
        target = layer(s)
        step = jnp.where(target > z, 1, -1)
        arrives_from_above = (target < z) & (z - 1 == target)
        slot = jnp.where(arrives_from_above, depth, target)
        span = pl.ds(q * chunk, chunk)
        return pltpu.make_async_remote_copy(
            src_ref=part.at[depth + s, span], dst_ref=from_z.at[slot, span], send_sem=z_send.at[s, q],
            recv_sem=z_recv.at[slot, q], device_id={"row": me + 4 * step}, device_id_type=MESH)

    def z_arrival(slot, q):
        span = pl.ds(q * chunk, chunk)
        return pltpu.make_async_remote_copy(
            src_ref=from_z.at[slot, span], dst_ref=from_z.at[slot, span], send_sem=z_send.at[0, q],
            recv_sem=z_recv.at[slot, q], device_id={"row": across}, device_id_type=MESH)

    b_local.start()
    for b in range(2 * depth):
        a_local(b).start()

    barrier = pltpu.get_barrier_semaphore()
    pl.semaphore_signal(barrier, inc=1, device_id={"row": sibling}, device_id_type=MESH)
    pl.semaphore_signal(barrier, inc=1, device_id={"row": across}, device_id_type=MESH)

    @pl.when(up)
    def _():
        pl.semaphore_signal(barrier, inc=1, device_id={"row": me + 4}, device_id_type=MESH)

    @pl.when(down)
    def _():
        pl.semaphore_signal(barrier, inc=1, device_id={"row": me - 4}, device_id_type=MESH)

    pl.semaphore_wait(barrier, 2 + jnp.where(up, 1, 0) + jnp.where(down, 1, 0))

    b_swap.start()
    for b in range(2 * depth):
        a_swap(b).start()

    block_of = lax.broadcasted_iota(jnp.int32, (TILE, width), 1) // TILE
    labels = jnp.zeros((TILE, width), jnp.int32)
    for j in range(width // TILE):
        labels = jnp.where(block_of == j, column_ref[j], labels)

    def mask(i, owner, base):
        span = pl.ds(pl.multiple_of(base + i * TILE, TILE), TILE)
        label = pair_ref[owner * (local_k // TILE) + i]
        kept = jnp.where(labels == label, b_buf[span, :], 0.0)
        b_high[span, :], b_low[span, :] = split(kept)

    b_local.wait()
    for i in range(local_k // TILE):
        mask(i, me, 0)
    b_swap.wait_recv()
    for i in range(local_k // TILE):
        mask(i, sibling, local_k)

    half = rows // 2

    def multiply(b, _):
        a_local(b).wait()
        a_swap(b).wait_recv()
        for t in range(2):
            high, low = split(a_buf[b, :, pl.ds(t * half, half)].T)
            dot = functools.partial(jnp.dot, preferred_element_type=jnp.float32)
            part[b, pl.ds(t * half, half), :] = (
                dot(high, b_high[...]) + dot(high, b_low[...]) + dot(low, b_high[...]))

            @pl.when(b < depth)
            def _():
                for q in range(t * CHUNKS // 2, (t + 1) * CHUNKS // 2):
                    y_copy(b, q).start()
        return 0

    lax.fori_loop(0, 2 * depth, multiply, 0)

    def forward(s, _):
        target = layer(s)
        fed = ((target > z) & down) | ((target < z) & up)
        for q in range(CHUNKS):
            span = pl.ds(q * chunk, chunk)
            y_copy(s, q).wait_recv()
            part[depth + s, span, :] += from_y[s, span, :]

            @pl.when(fed)
            def _():
                z_arrival(target, q).wait_recv()
                part[depth + s, span, :] += from_z[target, span, :]

            z_copy(s, q).start()
        return 0

    lax.fori_loop(0, depth - 1, forward, 0)

    last = depth - 1
    for q in range(CHUNKS):
        span = pl.ds(q * chunk, chunk)
        y_copy(last, q).wait_recv()
        out_ref[span, :] = part[depth + last, span, :] + from_y[last, span, :]

        @pl.when(down)
        def _():
            z_arrival(z, q).wait_recv()
            out_ref[span, :] += from_z[z, span, :]

        @pl.when(up)
        def _():
            z_arrival(depth, q).wait_recv()
            out_ref[span, :] += from_z[depth, span, :]

    b_swap.wait_send()

    def finish(s, _):
        a_swap(s).wait_send()
        a_swap(depth + s).wait_send()
        for q in range(CHUNKS):
            y_copy(s, q).wait_send()

            @pl.when(s < last)
            def _():
                z_copy(s, q).wait_send()
        return 0

    lax.fori_loop(0, depth, finish, 0)


def shards(devices, amplitudes, integrals, pair_irrep, column_irrep):
    depth = devices // 4
    local_k, local_m = amplitudes.shape
    width = integrals.shape[1]
    rows = local_m // devices
    scratch = [
        pltpu.VMEM((2 * depth, 2 * local_k, rows), jnp.float32),
        pltpu.VMEM((2 * local_k, width), jnp.float32),
        pltpu.VMEM((2 * local_k, width), jnp.bfloat16),
        pltpu.VMEM((2 * local_k, width), jnp.bfloat16),
        pltpu.VMEM((2 * depth, rows, width), jnp.float32),
        pltpu.VMEM((depth, rows, width), jnp.float32),
        pltpu.VMEM((depth + 1, rows, width), jnp.float32),
        pltpu.SemaphoreType.DMA((2 * depth,)),
        pltpu.SemaphoreType.DMA,
        pltpu.SemaphoreType.DMA((2 * depth,)),
        pltpu.SemaphoreType.DMA((2 * depth,)),
        pltpu.SemaphoreType.DMA,
        pltpu.SemaphoreType.DMA,
        pltpu.SemaphoreType.DMA((depth, CHUNKS)),
        pltpu.SemaphoreType.DMA((depth, CHUNKS)),
        pltpu.SemaphoreType.DMA((depth, CHUNKS)),
        pltpu.SemaphoreType.DMA((depth + 1, CHUNKS)),
    ]
    return pl.pallas_call(
        functools.partial(kernel, depth),
        out_shape=jax.ShapeDtypeStruct((rows, width), jnp.float32),
        in_specs=[
            pl.BlockSpec(memory_space=pl.ANY),
            pl.BlockSpec(memory_space=pl.ANY),
            pl.BlockSpec(memory_space=pltpu.SMEM),
            pl.BlockSpec(memory_space=pltpu.SMEM),
        ],
        out_specs=pl.BlockSpec(memory_space=pltpu.VMEM),
        scratch_shapes=scratch,
        cost_estimate=pl.CostEstimate(
            flops=12 * local_k * local_m * width, bytes_accessed=4 * local_k * (local_m + width), transcendentals=0),
        compiler_params=pltpu.CompilerParams(
            collective_id=0, has_side_effects=True, vmem_limit_bytes=60 * 1024 * 1024),
    )(amplitudes, integrals, pair_irrep, column_irrep)


def solution(mesh):
    placed = (P("row", "groups"), P("row", "groups"), P("groups"), P("groups"))
    return jax.shard_map(
        functools.partial(shards, mesh.shape["row"]), mesh=mesh, in_specs=placed, out_specs=P("row", "groups"),
        check_vma=False)
```

```python
import functools

import jax
import jax.numpy as jnp
from jax import lax
from jax.experimental import pallas as pl
from jax.experimental.pallas import tpu as pltpu
from jax.sharding import PartitionSpec as P

TILE = 64
MESH = pl.DeviceIdType.MESH
CHUNKS = 4
Z_FIRST = 3


def split(x):
    high = x.astype(jnp.bfloat16)
    low = (x - high.astype(jnp.float32)).astype(jnp.bfloat16)
    return high, low


def kernel(depth, a_hbm, b_hbm, pair_ref, column_ref, out_ref, a_buf, b_buf, b_high, b_low, part, from_y, from_z, early_z, early_y,
           a_sem, b_sem, a_send, a_recv, b_send, b_recv, y_send, y_recv, z_send, z_recv, ez_send, ez_recv, ey_send, ey_recv):
    local_k, width = b_hbm.shape
    rows = out_ref.shape[0]
    early = rows * Z_FIRST // 16
    chunk = (rows - early) // CHUNKS
    last = depth - 1
    tail = pl.ds(rows - early, early)
    me = lax.axis_index("row")
    z, y, c = me // 4, (me // 2) % 2, me % 2
    sibling = me + 1 - 2 * c
    across = me + 2 - 4 * y
    up, down = z < depth - 1, z > 0

    order = []
    low, high = z * 0, z * 0 + depth - 1
    for _ in range(depth):
        take_high = (high - z) > (z - low)
        order.append(jnp.where(take_high, high, low))
        low, high = jnp.where(take_high, low, low + 1), jnp.where(take_high, high - 1, high)

    def layer(s):
        found = order[0]
        for k in range(1, depth):
            found = jnp.where(s == k, order[k], found)
        return found

    def columns(b, core):
        other = 1 - b // depth
        side = y + other * (1 - 2 * y)
        owner = 4 * layer(b % depth) + 2 * side + core
        return pl.ds(pl.multiple_of(owner * rows, rows), rows)

    def slot_of(step):
        moved = jnp.where(step == 0, 0, jnp.where(step == 1, last, step - 1))
        return jnp.where(step < depth, moved, step)

    def a_local(b):
        return pltpu.make_async_copy(a_hbm.at[:, columns(b, c)], a_buf.at[b, pl.ds(0, local_k)], a_sem.at[b])

    def a_swap(b):
        return pltpu.make_async_remote_copy(
            src_ref=a_hbm.at[:, columns(b, 1 - c)], dst_ref=a_buf.at[b, pl.ds(local_k, local_k)],
            send_sem=a_send.at[b], recv_sem=a_recv.at[b], device_id={"row": sibling}, device_id_type=MESH)

    b_local = pltpu.make_async_copy(b_hbm, b_buf.at[pl.ds(0, local_k)], b_sem)
    b_swap = pltpu.make_async_remote_copy(
        src_ref=b_hbm, dst_ref=b_buf.at[pl.ds(local_k, local_k)], send_sem=b_send, recv_sem=b_recv,
        device_id={"row": sibling}, device_id_type=MESH)

    def y_copy(s, q):
        span = pl.ds(q * chunk, chunk)
        return pltpu.make_async_remote_copy(
            src_ref=part.at[s, span], dst_ref=from_y.at[s, span], send_sem=y_send.at[s, q], recv_sem=y_recv.at[s, q],
            device_id={"row": across}, device_id_type=MESH)

    def z_copy(s, q):
        target = layer(s)
        step = jnp.where(target > z, 1, -1)
        slot = landing(target)
        span = pl.ds(q * chunk, chunk)
        return pltpu.make_async_remote_copy(
            src_ref=part.at[depth + s, span], dst_ref=from_z.at[slot, span], send_sem=z_send.at[s, q],
            recv_sem=z_recv.at[slot, q], device_id={"row": me + 4 * step}, device_id_type=MESH)

    def landing(target):
        arrives_from_above = (target < z) & (z - 1 == target)
        return jnp.where(arrives_from_above, depth, target)

    def early_z_copy(side, s):
        target = layer(s)
        step = jnp.where(target > z, 1, -1)
        slot = side * (depth + 1) + landing(target)
        return pltpu.make_async_remote_copy(
            src_ref=part.at[side * depth + s, tail], dst_ref=early_z.at[slot], send_sem=ez_send.at[side * depth + s],
            recv_sem=ez_recv.at[slot], device_id={"row": me + 4 * step}, device_id_type=MESH)

    def early_z_arrival(slot):
        return pltpu.make_async_remote_copy(
            src_ref=early_z.at[slot], dst_ref=early_z.at[slot], send_sem=ez_send.at[0],
            recv_sem=ez_recv.at[slot], device_id={"row": across}, device_id_type=MESH)

    early_y_copy = pltpu.make_async_remote_copy(
        src_ref=part.at[last, tail], dst_ref=early_y, send_sem=ey_send, recv_sem=ey_recv,
        device_id={"row": across}, device_id_type=MESH)

    def z_arrival(slot, q):
        span = pl.ds(q * chunk, chunk)
        return pltpu.make_async_remote_copy(
            src_ref=from_z.at[slot, span], dst_ref=from_z.at[slot, span], send_sem=z_send.at[0, q],
            recv_sem=z_recv.at[slot, q], device_id={"row": across}, device_id_type=MESH)

    b_local.start()
    for step in range(2 * depth):
        a_local(slot_of(step)).start()

    barrier = pltpu.get_barrier_semaphore()
    pl.semaphore_signal(barrier, inc=1, device_id={"row": sibling}, device_id_type=MESH)
    pl.semaphore_signal(barrier, inc=1, device_id={"row": across}, device_id_type=MESH)

    @pl.when(up)
    def _():
        pl.semaphore_signal(barrier, inc=1, device_id={"row": me + 4}, device_id_type=MESH)

    @pl.when(down)
    def _():
        pl.semaphore_signal(barrier, inc=1, device_id={"row": me - 4}, device_id_type=MESH)

    pl.semaphore_wait(barrier, 2 + jnp.where(up, 1, 0) + jnp.where(down, 1, 0))

    b_swap.start()
    for step in range(2 * depth):
        a_swap(slot_of(step)).start()

    block_of = lax.broadcasted_iota(jnp.int32, (TILE, width), 1) // TILE
    labels = jnp.zeros((TILE, width), jnp.int32)
    for j in range(width // TILE):
        labels = jnp.where(block_of == j, column_ref[j], labels)

    def mask(i, owner, base):
        span = pl.ds(pl.multiple_of(base + i * TILE, TILE), TILE)
        label = pair_ref[owner * (local_k // TILE) + i]
        kept = jnp.where(labels == label, b_buf[span, :], 0.0)
        b_high[span, :], b_low[span, :] = split(kept)

    b_local.wait()
    for i in range(local_k // TILE):
        mask(i, me, 0)
    b_swap.wait_recv()
    for i in range(local_k // TILE):
        mask(i, sibling, local_k)

    half = rows // 2

    def is_fed(s):
        target = layer(s)
        return ((target > z) & down) | ((target < z) & up)

    def multiply(step, _):
        b = slot_of(step)
        a_local(b).wait()
        a_swap(b).wait_recv()
        for t in range(2):
            high, low = split(a_buf[b, :, pl.ds(t * half, half)].T)
            dot = functools.partial(jnp.dot, preferred_element_type=jnp.float32)
            part[b, pl.ds(t * half, half), :] = (
                dot(high, b_high[...]) + dot(high, b_low[...]) + dot(low, b_high[...]))

            @pl.when(step < depth)
            def _():
                for q in range(t * CHUNKS // 2, (t + 1) * CHUNKS // 2):
                    y_copy(b, q).start()

        side, s = b // depth, b % depth

        @pl.when((s < last) & jnp.logical_not(is_fed(s)))
        def _():
            early_z_copy(side, s).start()
        return 0

    lax.fori_loop(0, 2 * depth, multiply, 0)

    def early_forward(s, _):
        @pl.when(is_fed(s))
        def _():
            for side in range(2):
                slot = side * (depth + 1) + layer(s)
                early_z_arrival(slot).wait_recv()
                part[side * depth + s, tail, :] += early_z[slot]
                early_z_copy(side, s).start()
        return 0

    lax.fori_loop(0, last, early_forward, 0)

    def forward(s, _):
        fed = is_fed(s)
        target = layer(s)
        for q in range(CHUNKS):
            span = pl.ds(q * chunk, chunk)
            y_copy(s, q).wait_recv()
            part[depth + s, span, :] += from_y[s, span, :]

            @pl.when(fed)
            def _():
                z_arrival(target, q).wait_recv()
                part[depth + s, span, :] += from_z[target, span, :]

            z_copy(s, q).start()
        return 0

    forward(0, 0)

    for side in range(2):
        @pl.when(down)
        def _():
            slot = side * (depth + 1) + z
            early_z_arrival(slot).wait_recv()
            part[side * depth + last, tail, :] += early_z[slot]

        @pl.when(up)
        def _():
            slot = side * (depth + 1) + depth
            early_z_arrival(slot).wait_recv()
            part[side * depth + last, tail, :] += early_z[slot]

        if side == 0:
            early_y_copy.start()

    lax.fori_loop(1, last, forward, 0)

    for q in range(CHUNKS):
        span = pl.ds(q * chunk, chunk)
        y_copy(last, q).wait_recv()
        out_ref[span, :] = part[depth + last, span, :] + from_y[last, span, :]

        @pl.when(down)
        def _():
            z_arrival(z, q).wait_recv()
            out_ref[span, :] += from_z[z, span, :]

        @pl.when(up)
        def _():
            z_arrival(depth, q).wait_recv()
            out_ref[span, :] += from_z[depth, span, :]

    early_y_copy.wait_recv()
    out_ref[tail, :] = part[depth + last, tail, :] + early_y[...]
    early_y_copy.wait_send()
    b_swap.wait_send()

    def finish(s, _):
        a_swap(s).wait_send()
        a_swap(depth + s).wait_send()
        for q in range(CHUNKS):
            y_copy(s, q).wait_send()

            @pl.when(s < last)
            def _():
                z_copy(s, q).wait_send()

        @pl.when(s < last)
        def _():
            early_z_copy(0, s).wait_send()
            early_z_copy(1, s).wait_send()
        return 0

    lax.fori_loop(0, depth, finish, 0)


def shards(devices, amplitudes, integrals, pair_irrep, column_irrep):
    depth = devices // 4
    local_k, local_m = amplitudes.shape
    width = integrals.shape[1]
    rows = local_m // devices
    early = rows * Z_FIRST // 16
    scratch = [
        pltpu.VMEM((2 * depth, 2 * local_k, rows), jnp.float32),
        pltpu.VMEM((2 * local_k, width), jnp.float32),
        pltpu.VMEM((2 * local_k, width), jnp.bfloat16),
        pltpu.VMEM((2 * local_k, width), jnp.bfloat16),
        pltpu.VMEM((2 * depth, rows, width), jnp.float32),
        pltpu.VMEM((depth, rows, width), jnp.float32),
        pltpu.VMEM((depth + 1, rows, width), jnp.float32),
        pltpu.VMEM((2 * (depth + 1), early, width), jnp.float32),
        pltpu.VMEM((early, width), jnp.float32),
        pltpu.SemaphoreType.DMA((2 * depth,)),
        pltpu.SemaphoreType.DMA,
        pltpu.SemaphoreType.DMA((2 * depth,)),
        pltpu.SemaphoreType.DMA((2 * depth,)),
        pltpu.SemaphoreType.DMA,
        pltpu.SemaphoreType.DMA,
        pltpu.SemaphoreType.DMA((depth, CHUNKS)),
        pltpu.SemaphoreType.DMA((depth, CHUNKS)),
        pltpu.SemaphoreType.DMA((depth, CHUNKS)),
        pltpu.SemaphoreType.DMA((depth + 1, CHUNKS)),
        pltpu.SemaphoreType.DMA((2 * depth,)),
        pltpu.SemaphoreType.DMA((2 * (depth + 1),)),
        pltpu.SemaphoreType.DMA,
        pltpu.SemaphoreType.DMA,
    ]
    return pl.pallas_call(
        functools.partial(kernel, depth),
        out_shape=jax.ShapeDtypeStruct((rows, width), jnp.float32),
        in_specs=[
            pl.BlockSpec(memory_space=pl.ANY),
            pl.BlockSpec(memory_space=pl.ANY),
            pl.BlockSpec(memory_space=pltpu.SMEM),
            pl.BlockSpec(memory_space=pltpu.SMEM),
        ],
        out_specs=pl.BlockSpec(memory_space=pltpu.VMEM),
        scratch_shapes=scratch,
        cost_estimate=pl.CostEstimate(
            flops=12 * local_k * local_m * width, bytes_accessed=4 * local_k * (local_m + width), transcendentals=0),
        compiler_params=pltpu.CompilerParams(
            collective_id=0, has_side_effects=True, vmem_limit_bytes=60 * 1024 * 1024),
    )(amplitudes, integrals, pair_irrep, column_irrep)


def solution(mesh):
    placed = (P("row", "groups"), P("row", "groups"), P("groups"), P("groups"))
    return jax.shard_map(
        functools.partial(shards, mesh.shape["row"]), mesh=mesh, in_specs=placed, out_specs=P("row", "groups"),
        check_vma=False)
```

```python
import functools

import jax
import jax.numpy as jnp
from jax import lax
from jax.experimental import pallas as pl
from jax.experimental.pallas import tpu as pltpu
from jax.sharding import PartitionSpec as P

TILE = 64
MESH = pl.DeviceIdType.MESH
BOUNDS = (10, 20, 32, 44, 56, 64)
CHUNKS = len(BOUNDS) - 1
OWN_AT = 3
AHEAD = 1


def split(x):
    high = x.astype(jnp.bfloat16)
    low = (x - high.astype(jnp.float32)).astype(jnp.bfloat16)
    return high, low


def kernel(depth, a_hbm, b_hbm, pair_ref, column_ref, out_ref, a_buf, b_buf, b_high, b_low, part, from_y, from_z, early_z, early_y,
           a_sem, b_sem, a_send, a_recv, b_send, b_recv, y_send, y_recv, z_send, z_recv, ez_send, ez_recv, ey_send, ey_recv):
    local_k, width = b_hbm.shape
    rows = out_ref.shape[0]
    bounds = [rows * bound // 64 for bound in BOUNDS]
    spans = [pl.ds(start, end - start) for start, end in zip(bounds, bounds[1:])]
    head = pl.ds(0, bounds[0])
    half = rows // 2
    last = depth - 1
    me = lax.axis_index("row")
    z, y, c = me // 4, (me // 2) % 2, me % 2
    sibling = me + 1 - 2 * c
    across = me + 2 - 4 * y
    up, down = z < depth - 1, z > 0

    order = []
    low, high = z * 0, z * 0 + depth - 1
    for _ in range(depth):
        take_high = (high - z) > (z - low)
        order.append(jnp.where(take_high, high, low))
        low, high = jnp.where(take_high, low, low + 1), jnp.where(take_high, high - 1, high)

    def layer(s):
        found = order[0]
        for k in range(1, depth):
            found = jnp.where(s == k, order[k], found)
        return found

    def columns(b, core, t):
        other = 1 - b // depth
        side = y + other * (1 - 2 * y)
        owner = 4 * layer(b % depth) + 2 * side + core
        return pl.ds(pl.multiple_of(owner * rows + t * half, half), half)

    def slot_of(step):
        moved = jnp.where(step < OWN_AT, step, jnp.where(step == OWN_AT, last, step - 1))
        return jnp.where(step < depth, moved, step)

    def a_local(b, t):
        return pltpu.make_async_copy(
            a_hbm.at[:, columns(b, c, t)], a_buf.at[b, t, pl.ds(0, local_k)], a_sem.at[b, t])

    def a_swap(b, t):
        return pltpu.make_async_remote_copy(
            src_ref=a_hbm.at[:, columns(b, 1 - c, t)], dst_ref=a_buf.at[b, t, pl.ds(local_k, local_k)],
            send_sem=a_send.at[b, t], recv_sem=a_recv.at[b, t], device_id={"row": sibling}, device_id_type=MESH)

    b_local = pltpu.make_async_copy(b_hbm, b_buf.at[pl.ds(0, local_k)], b_sem)
    b_swap = pltpu.make_async_remote_copy(
        src_ref=b_hbm, dst_ref=b_buf.at[pl.ds(local_k, local_k)], send_sem=b_send, recv_sem=b_recv,
        device_id={"row": sibling}, device_id_type=MESH)

    def y_copy(s, q):
        span = spans[q]
        return pltpu.make_async_remote_copy(
            src_ref=part.at[s, span], dst_ref=from_y.at[s, span], send_sem=y_send.at[s, q], recv_sem=y_recv.at[s, q],
            device_id={"row": across}, device_id_type=MESH)

    def z_copy(s, q):
        target = layer(s)
        step = jnp.where(target > z, 1, -1)
        slot = landing(target)
        span = spans[q]
        return pltpu.make_async_remote_copy(
            src_ref=part.at[depth + s, span], dst_ref=from_z.at[slot, span], send_sem=z_send.at[s, q],
            recv_sem=z_recv.at[slot, q], device_id={"row": me + 4 * step}, device_id_type=MESH)

    def landing(target):
        arrives_from_above = (target < z) & (z - 1 == target)
        return jnp.where(arrives_from_above, depth, target)

    def early_z_copy(side, s):
        target = layer(s)
        step = jnp.where(target > z, 1, -1)
        slot = side * (depth + 1) + landing(target)
        return pltpu.make_async_remote_copy(
            src_ref=part.at[side * depth + s, head], dst_ref=early_z.at[slot], send_sem=ez_send.at[side * depth + s],
            recv_sem=ez_recv.at[slot], device_id={"row": me + 4 * step}, device_id_type=MESH)

    def early_z_arrival(slot):
        return pltpu.make_async_remote_copy(
            src_ref=early_z.at[slot], dst_ref=early_z.at[slot], send_sem=ez_send.at[0],
            recv_sem=ez_recv.at[slot], device_id={"row": across}, device_id_type=MESH)

    early_y_copy = pltpu.make_async_remote_copy(
        src_ref=part.at[last, head], dst_ref=early_y, send_sem=ey_send, recv_sem=ey_recv,
        device_id={"row": across}, device_id_type=MESH)

    def z_arrival(slot, q):
        span = spans[q]
        return pltpu.make_async_remote_copy(
            src_ref=from_z.at[slot, span], dst_ref=from_z.at[slot, span], send_sem=z_send.at[0, q],
            recv_sem=z_recv.at[slot, q], device_id={"row": across}, device_id_type=MESH)

    b_local.start()
    for step in range(2 * depth):
        for t in range(2):
            a_local(slot_of(step), t).start()

    barrier = pltpu.get_barrier_semaphore()
    pl.semaphore_signal(barrier, inc=1, device_id={"row": sibling}, device_id_type=MESH)
    pl.semaphore_signal(barrier, inc=1, device_id={"row": across}, device_id_type=MESH)

    @pl.when(up)
    def _():
        pl.semaphore_signal(barrier, inc=1, device_id={"row": me + 4}, device_id_type=MESH)

    @pl.when(down)
    def _():
        pl.semaphore_signal(barrier, inc=1, device_id={"row": me - 4}, device_id_type=MESH)

    pl.semaphore_wait(barrier, 2 + jnp.where(up, 1, 0) + jnp.where(down, 1, 0))

    b_swap.start()
    for step in range(AHEAD):
        for t in range(2):
            a_swap(slot_of(step), t).start()

    block_of = lax.broadcasted_iota(jnp.int32, (TILE, width), 1) // TILE
    labels = jnp.zeros((TILE, width), jnp.int32)
    for j in range(width // TILE):
        labels = jnp.where(block_of == j, column_ref[j], labels)

    def mask(i, owner, base):
        span = pl.ds(pl.multiple_of(base + i * TILE, TILE), TILE)
        label = pair_ref[owner * (local_k // TILE) + i]
        kept = jnp.where(labels == label, b_buf[span, :], 0.0)
        b_high[span, :], b_low[span, :] = split(kept)

    b_local.wait()
    for i in range(local_k // TILE):
        mask(i, me, 0)
    b_swap.wait_recv()
    for i in range(local_k // TILE):
        mask(i, sibling, local_k)

    def is_fed(s):
        target = layer(s)
        return ((target > z) & down) | ((target < z) & up)

    def multiply(step, _):
        b = slot_of(step)

        @pl.when(step < 2 * depth - AHEAD)
        def _():
            for t in range(2):
                a_swap(slot_of(step + AHEAD), t).start()

        side, s = b // depth, b % depth
        for t in range(2):
            a_local(b, t).wait()
            a_swap(b, t).wait_recv()
            high, low = split(a_buf[b, t].T)
            dot = functools.partial(jnp.dot, preferred_element_type=jnp.float32)
            part[b, pl.ds(t * half, half), :] = (
                dot(high, b_high[...]) + dot(high, b_low[...]) + dot(low, b_high[...]))

            if t == 0:
                @pl.when((s < last) & jnp.logical_not(is_fed(s)))
                def _():
                    early_z_copy(side, s).start()

            @pl.when(step < depth)
            def _():
                for q in range(CHUNKS):
                    if bounds[q + 1] <= half * (t + 1) and bounds[q + 1] > half * t:
                        y_copy(b, q).start()

        return 0

    lax.fori_loop(0, 2 * depth, multiply, 0)

    def early_forward(s, _):
        @pl.when(is_fed(s))
        def _():
            for side in range(2):
                slot = side * (depth + 1) + layer(s)
                early_z_arrival(slot).wait_recv()
                part[side * depth + s, head, :] += early_z[slot]
                early_z_copy(side, s).start()
        return 0

    lax.fori_loop(0, last, early_forward, 0)

    def forward(s, _):
        fed = is_fed(s)
        target = layer(s)
        for q in range(CHUNKS):
            span = spans[q]
            y_copy(s, q).wait_recv()
            part[depth + s, span, :] += from_y[s, span, :]

            @pl.when(fed)
            def _():
                z_arrival(target, q).wait_recv()
                part[depth + s, span, :] += from_z[target, span, :]

            z_copy(s, q).start()
        return 0

    forward(0, 0)

    for side in range(2):
        @pl.when(down)
        def _():
            slot = side * (depth + 1) + z
            early_z_arrival(slot).wait_recv()
            part[side * depth + last, head, :] += early_z[slot]

        @pl.when(up)
        def _():
            slot = side * (depth + 1) + depth
            early_z_arrival(slot).wait_recv()
            part[side * depth + last, head, :] += early_z[slot]

        if side == 0:
            early_y_copy.start()

    lax.fori_loop(1, last, forward, 0)

    for q in range(CHUNKS):
        span = spans[q]
        y_copy(last, q).wait_recv()
        out_ref[span, :] = part[depth + last, span, :] + from_y[last, span, :]

        @pl.when(down)
        def _():
            z_arrival(z, q).wait_recv()
            out_ref[span, :] += from_z[z, span, :]

        @pl.when(up)
        def _():
            z_arrival(depth, q).wait_recv()
            out_ref[span, :] += from_z[depth, span, :]

    early_y_copy.wait_recv()
    out_ref[head, :] = part[depth + last, head, :] + early_y[...]
    early_y_copy.wait_send()
    b_swap.wait_send()

    def finish(s, _):
        for t in range(2):
            a_swap(s, t).wait_send()
            a_swap(depth + s, t).wait_send()
        for q in range(CHUNKS):
            y_copy(s, q).wait_send()

            @pl.when(s < last)
            def _():
                z_copy(s, q).wait_send()

        @pl.when(s < last)
        def _():
            early_z_copy(0, s).wait_send()
            early_z_copy(1, s).wait_send()
        return 0

    lax.fori_loop(0, depth, finish, 0)


def shards(devices, amplitudes, integrals, pair_irrep, column_irrep):
    depth = devices // 4
    local_k, local_m = amplitudes.shape
    width = integrals.shape[1]
    rows = local_m // devices
    early = rows * BOUNDS[0] // 64
    scratch = [
        pltpu.VMEM((2 * depth, 2, 2 * local_k, rows // 2), jnp.float32),
        pltpu.VMEM((2 * local_k, width), jnp.float32),
        pltpu.VMEM((2 * local_k, width), jnp.bfloat16),
        pltpu.VMEM((2 * local_k, width), jnp.bfloat16),
        pltpu.VMEM((2 * depth, rows, width), jnp.float32),
        pltpu.VMEM((depth, rows, width), jnp.float32),
        pltpu.VMEM((depth + 1, rows, width), jnp.float32),
        pltpu.VMEM((2 * (depth + 1), early, width), jnp.float32),
        pltpu.VMEM((early, width), jnp.float32),
        pltpu.SemaphoreType.DMA((2 * depth, 2)),
        pltpu.SemaphoreType.DMA,
        pltpu.SemaphoreType.DMA((2 * depth, 2)),
        pltpu.SemaphoreType.DMA((2 * depth, 2)),
        pltpu.SemaphoreType.DMA,
        pltpu.SemaphoreType.DMA,
        pltpu.SemaphoreType.DMA((depth, CHUNKS)),
        pltpu.SemaphoreType.DMA((depth, CHUNKS)),
        pltpu.SemaphoreType.DMA((depth, CHUNKS)),
        pltpu.SemaphoreType.DMA((depth + 1, CHUNKS)),
        pltpu.SemaphoreType.DMA((2 * depth,)),
        pltpu.SemaphoreType.DMA((2 * (depth + 1),)),
        pltpu.SemaphoreType.DMA,
        pltpu.SemaphoreType.DMA,
    ]
    return pl.pallas_call(
        functools.partial(kernel, depth),
        out_shape=pltpu.VMEM((rows, width), jnp.float32),
        in_specs=[
            pl.BlockSpec(memory_space=pl.ANY),
            pl.BlockSpec(memory_space=pl.ANY),
            pl.BlockSpec(memory_space=pltpu.SMEM),
            pl.BlockSpec(memory_space=pltpu.SMEM),
        ],
        out_specs=pl.BlockSpec(memory_space=pltpu.VMEM),
        scratch_shapes=scratch,
        cost_estimate=pl.CostEstimate(
            flops=12 * local_k * local_m * width, bytes_accessed=4 * local_k * (local_m + width), transcendentals=0),
        compiler_params=pltpu.CompilerParams(
            collective_id=0, has_side_effects=True, vmem_limit_bytes=60 * 1024 * 1024),
    )(amplitudes, integrals, pair_irrep, column_irrep)


def solution(mesh):
    placed = (P("row", "groups"), P("row", "groups"), P("groups"), P("groups"))
    return jax.shard_map(
        functools.partial(shards, mesh.shape["row"]), mesh=mesh, in_specs=placed, out_specs=P("row", "groups"),
        check_vma=False)
```

```python
import functools

import jax
import jax.numpy as jnp
from jax import lax
from jax.experimental import pallas as pl
from jax.experimental.pallas import tpu as pltpu
from jax.sharding import PartitionSpec as P

TILE = 64
MESH = pl.DeviceIdType.MESH
BOUNDS = (11, 20, 32, 44, 56, 64)
CHUNKS = len(BOUNDS) - 1
OWN_AT = 3


def split(x):
    high = x.astype(jnp.bfloat16)
    low = (x - high.astype(jnp.float32)).astype(jnp.bfloat16)
    return high, low


def kernel(depth, a_hbm, b_hbm, pair_ref, column_ref, out_ref, a_buf, b_buf, b_high, b_low, part, from_y, from_z, early_z, early_y,
           a_cross, cross_out, cross_in,
           a_sem, b_sem, a_send, a_recv, b_send, b_recv, y_send, y_recv, z_send, z_recv, ez_send, ez_recv, ey_send, ey_recv,
           ac_sem, c_send, c_recv):
    local_k, width = b_hbm.shape
    rows = out_ref.shape[0]
    bounds = [rows * bound // 64 for bound in BOUNDS]
    spans = [pl.ds(start, end - start) for start, end in zip(bounds, bounds[1:])]
    head = pl.ds(0, bounds[0])
    half = rows // 2
    last = depth - 1
    me = lax.axis_index("row")
    z, y, c = me // 4, (me // 2) % 2, me % 2
    sibling = me + 1 - 2 * c
    across = me + 2 - 4 * y
    up, down = z < depth - 1, z > 0

    order = []
    low, high = z * 0, z * 0 + depth - 1
    for _ in range(depth):
        take_high = (high - z) > (z - low)
        order.append(jnp.where(take_high, high, low))
        low, high = jnp.where(take_high, low, low + 1), jnp.where(take_high, high - 1, high)

    def layer(s):
        found = order[0]
        for k in range(1, depth):
            found = jnp.where(s == k, order[k], found)
        return found

    def columns(b, core, t):
        other = 1 - b // depth
        side = y + other * (1 - 2 * y)
        owner = 4 * layer(b % depth) + 2 * side + core
        return pl.ds(pl.multiple_of(owner * rows + t * half, half), half)

    def slot_of(step):
        moved = jnp.where(step < OWN_AT, step, jnp.where(step == OWN_AT, last, step - 1))
        return jnp.where(step < depth, moved, step)

    def a_local(b, t):
        return pltpu.make_async_copy(
            a_hbm.at[:, columns(b, c, t)], a_buf.at[b, t, pl.ds(0, local_k)], a_sem.at[b, t])

    def a_swap(b, t):
        return pltpu.make_async_remote_copy(
            src_ref=a_hbm.at[:, columns(b, 1 - c, t)], dst_ref=a_buf.at[b, t, pl.ds(local_k, local_k)],
            send_sem=a_send.at[b, t], recv_sem=a_recv.at[b, t], device_id={"row": sibling}, device_id_type=MESH)

    pieces = [(start, end) for start, end in zip([0] + bounds, bounds) if end <= half]
    a_other = pltpu.make_async_copy(a_hbm.at[:, columns(0, 1 - c, 0)], a_cross, ac_sem)

    def cross(p):
        start, end = pieces[p]
        span = pl.ds(start, end - start)
        return pltpu.make_async_remote_copy(
            src_ref=cross_out.at[span], dst_ref=cross_in.at[span], send_sem=c_send.at[p], recv_sem=c_recv.at[p],
            device_id={"row": sibling}, device_id_type=MESH)

    b_local = pltpu.make_async_copy(b_hbm, b_buf.at[pl.ds(0, local_k)], b_sem)
    b_swap = pltpu.make_async_remote_copy(
        src_ref=b_hbm, dst_ref=b_buf.at[pl.ds(local_k, local_k)], send_sem=b_send, recv_sem=b_recv,
        device_id={"row": sibling}, device_id_type=MESH)

    def y_copy(s, q):
        span = spans[q]
        return pltpu.make_async_remote_copy(
            src_ref=part.at[s, span], dst_ref=from_y.at[s, span], send_sem=y_send.at[s, q], recv_sem=y_recv.at[s, q],
            device_id={"row": across}, device_id_type=MESH)

    def z_copy(s, q):
        target = layer(s)
        step = jnp.where(target > z, 1, -1)
        slot = landing(target)
        span = spans[q]
        return pltpu.make_async_remote_copy(
            src_ref=part.at[depth + s, span], dst_ref=from_z.at[slot, span], send_sem=z_send.at[s, q],
            recv_sem=z_recv.at[slot, q], device_id={"row": me + 4 * step}, device_id_type=MESH)

    def landing(target):
        arrives_from_above = (target < z) & (z - 1 == target)
        return jnp.where(arrives_from_above, depth, target)

    def early_z_copy(side, s):
        target = layer(s)
        step = jnp.where(target > z, 1, -1)
        slot = side * (depth + 1) + landing(target)
        return pltpu.make_async_remote_copy(
            src_ref=part.at[side * depth + s, head], dst_ref=early_z.at[slot], send_sem=ez_send.at[side * depth + s],
            recv_sem=ez_recv.at[slot], device_id={"row": me + 4 * step}, device_id_type=MESH)

    def early_z_arrival(slot):
        return pltpu.make_async_remote_copy(
            src_ref=early_z.at[slot], dst_ref=early_z.at[slot], send_sem=ez_send.at[0],
            recv_sem=ez_recv.at[slot], device_id={"row": across}, device_id_type=MESH)

    early_y_copy = pltpu.make_async_remote_copy(
        src_ref=part.at[last, head], dst_ref=early_y, send_sem=ey_send, recv_sem=ey_recv,
        device_id={"row": across}, device_id_type=MESH)

    def z_arrival(slot, q):
        span = spans[q]
        return pltpu.make_async_remote_copy(
            src_ref=from_z.at[slot, span], dst_ref=from_z.at[slot, span], send_sem=z_send.at[0, q],
            recv_sem=z_recv.at[slot, q], device_id={"row": across}, device_id_type=MESH)

    barrier = pltpu.get_barrier_semaphore()
    pl.semaphore_signal(barrier, inc=1, device_id={"row": sibling}, device_id_type=MESH)
    pl.semaphore_signal(barrier, inc=1, device_id={"row": across}, device_id_type=MESH)

    @pl.when(up)
    def _():
        pl.semaphore_signal(barrier, inc=1, device_id={"row": me + 4}, device_id_type=MESH)

    @pl.when(down)
    def _():
        pl.semaphore_signal(barrier, inc=1, device_id={"row": me - 4}, device_id_type=MESH)

    b_local.start()
    a_other.start()
    a_local(0, 0).start()
    a_local(0, 1).start()
    block_of = lax.broadcasted_iota(jnp.int32, (TILE, width), 1) // TILE
    labels = jnp.zeros((TILE, width), jnp.int32)
    for j in range(width // TILE):
        labels = jnp.where(block_of == j, column_ref[j], labels)

    def mask(i, owner, base):
        span = pl.ds(pl.multiple_of(base + i * TILE, TILE), TILE)
        label = pair_ref[owner * (local_k // TILE) + i]
        kept = jnp.where(labels == label, b_buf[span, :], 0.0)
        b_high[span, :], b_low[span, :] = split(kept)

    b_local.wait()
    for i in range(local_k // TILE):
        mask(i, me, 0)
    def product(x, span):
        high, low = split(x.T)
        dot = functools.partial(jnp.dot, preferred_element_type=jnp.float32)
        return dot(high, b_high[span, :]) + dot(high, b_low[span, :]) + dot(low, b_high[span, :])

    own, both = pl.ds(0, local_k), pl.ds(0, 2 * local_k)
    a_other.wait()
    cross_out[...] = product(a_cross[...], own)

    pl.semaphore_wait(barrier, 2 + jnp.where(up, 1, 0) + jnp.where(down, 1, 0))

    for p in range(len(pieces)):
        cross(p).start()
    b_swap.start()
    a_swap(0, 1).start()
    for step in range(1, 2 * depth):
        for t in range(2):
            a_local(slot_of(step), t).start()

    def is_fed(s):
        target = layer(s)
        return ((target > z) & down) | ((target < z) & up)

    a_local(0, 0).wait()
    part[0, pl.ds(0, half), :] = product(a_buf[0, 0, own, :], own)
    for p, (start, end) in enumerate(pieces):
        span = pl.ds(start, end - start)
        cross(p).wait_recv()
        part[0, span, :] += cross_in[span, :]
        if p == 0:
            @pl.when(jnp.logical_not(is_fed(0)))
            def _():
                early_z_copy(0, 0).start()
        else:
            y_copy(0, p - 1).start()

    b_swap.wait_recv()
    for i in range(local_k // TILE):
        mask(i, sibling, local_k)

    def tile(step, b, t):
        side, s = b // depth, b % depth
        a_local(b, t).wait()
        a_swap(b, t).wait_recv()
        part[b, pl.ds(t * half, half), :] = product(a_buf[b, t], both)

        if t == 0:
            @pl.when((s < last) & jnp.logical_not(is_fed(s)))
            def _():
                early_z_copy(side, s).start()

        @pl.when(step < depth)
        def _():
            for q in range(CHUNKS):
                if half * t < bounds[q + 1] <= half * (t + 1):
                    y_copy(b, q).start()

    def swap_next(step):
        for t in range(2):
            a_swap(slot_of(step + 1), t).start()

    def multiply(step, _):
        @pl.when(step < 2 * depth - 1)
        def _():
            swap_next(step)

        for t in range(2):
            tile(step, slot_of(step), t)
        return 0

    swap_next(0)
    tile(0, 0, 1)
    lax.fori_loop(1, 2 * depth, multiply, 0)

    def early_forward(s, _):
        @pl.when(is_fed(s))
        def _():
            for side in range(2):
                slot = side * (depth + 1) + layer(s)
                early_z_arrival(slot).wait_recv()
                part[side * depth + s, head, :] += early_z[slot]
                early_z_copy(side, s).start()
        return 0

    lax.fori_loop(0, last, early_forward, 0)

    def forward(s, _):
        fed = is_fed(s)
        target = layer(s)
        for q in range(CHUNKS):
            span = spans[q]
            y_copy(s, q).wait_recv()
            part[depth + s, span, :] += from_y[s, span, :]

            @pl.when(fed)
            def _():
                z_arrival(target, q).wait_recv()
                part[depth + s, span, :] += from_z[target, span, :]

            z_copy(s, q).start()
        return 0

    forward(0, 0)

    for side in range(2):
        @pl.when(down)
        def _():
            slot = side * (depth + 1) + z
            early_z_arrival(slot).wait_recv()
            part[side * depth + last, head, :] += early_z[slot]

        @pl.when(up)
        def _():
            slot = side * (depth + 1) + depth
            early_z_arrival(slot).wait_recv()
            part[side * depth + last, head, :] += early_z[slot]

        if side == 0:
            early_y_copy.start()

    lax.fori_loop(1, last, forward, 0)

    for q in range(CHUNKS):
        span = spans[q]
        y_copy(last, q).wait_recv()
        out_ref[span, :] = part[depth + last, span, :] + from_y[last, span, :]

        @pl.when(down)
        def _():
            z_arrival(z, q).wait_recv()
            out_ref[span, :] += from_z[z, span, :]

        @pl.when(up)
        def _():
            z_arrival(depth, q).wait_recv()
            out_ref[span, :] += from_z[depth, span, :]

    early_y_copy.wait_recv()
    out_ref[head, :] = part[depth + last, head, :] + early_y[...]
    early_y_copy.wait_send()
    for p in range(len(pieces)):
        cross(p).wait_send()
    b_swap.wait_send()

    def finish(s, _):
        @pl.when(s > 0)
        def _():
            a_swap(s, 0).wait_send()

        a_swap(s, 1).wait_send()
        for t in range(2):
            a_swap(depth + s, t).wait_send()
        for q in range(CHUNKS):
            y_copy(s, q).wait_send()

            @pl.when(s < last)
            def _():
                z_copy(s, q).wait_send()

        @pl.when(s < last)
        def _():
            early_z_copy(0, s).wait_send()
            early_z_copy(1, s).wait_send()
        return 0

    lax.fori_loop(0, depth, finish, 0)


def shards(devices, amplitudes, integrals, pair_irrep, column_irrep):
    depth = devices // 4
    local_k, local_m = amplitudes.shape
    width = integrals.shape[1]
    rows = local_m // devices
    early = rows * BOUNDS[0] // 64
    scratch = [
        pltpu.VMEM((2 * depth, 2, 2 * local_k, rows // 2), jnp.float32),
        pltpu.VMEM((2 * local_k, width), jnp.float32),
        pltpu.VMEM((2 * local_k, width), jnp.bfloat16),
        pltpu.VMEM((2 * local_k, width), jnp.bfloat16),
        pltpu.VMEM((2 * depth, rows, width), jnp.float32),
        pltpu.VMEM((depth, rows, width), jnp.float32),
        pltpu.VMEM((depth + 1, rows, width), jnp.float32),
        pltpu.VMEM((2 * (depth + 1), early, width), jnp.float32),
        pltpu.VMEM((early, width), jnp.float32),
        pltpu.VMEM((local_k, rows // 2), jnp.float32),
        pltpu.VMEM((rows // 2, width), jnp.float32),
        pltpu.VMEM((rows // 2, width), jnp.float32),
        pltpu.SemaphoreType.DMA((2 * depth, 2)),
        pltpu.SemaphoreType.DMA,
        pltpu.SemaphoreType.DMA((2 * depth, 2)),
        pltpu.SemaphoreType.DMA((2 * depth, 2)),
        pltpu.SemaphoreType.DMA,
        pltpu.SemaphoreType.DMA,
        pltpu.SemaphoreType.DMA((depth, CHUNKS)),
        pltpu.SemaphoreType.DMA((depth, CHUNKS)),
        pltpu.SemaphoreType.DMA((depth, CHUNKS)),
        pltpu.SemaphoreType.DMA((depth + 1, CHUNKS)),
        pltpu.SemaphoreType.DMA((2 * depth,)),
        pltpu.SemaphoreType.DMA((2 * (depth + 1),)),
        pltpu.SemaphoreType.DMA,
        pltpu.SemaphoreType.DMA,
        pltpu.SemaphoreType.DMA,
        pltpu.SemaphoreType.DMA((CHUNKS,)),
        pltpu.SemaphoreType.DMA((CHUNKS,)),
    ]
    return pl.pallas_call(
        functools.partial(kernel, depth),
        out_shape=pltpu.VMEM((rows, width), jnp.float32),
        in_specs=[
            pl.BlockSpec(memory_space=pl.ANY),
            pl.BlockSpec(memory_space=pl.ANY),
            pl.BlockSpec(memory_space=pltpu.SMEM),
            pl.BlockSpec(memory_space=pltpu.SMEM),
        ],
        out_specs=pl.BlockSpec(memory_space=pltpu.VMEM),
        scratch_shapes=scratch,
        cost_estimate=pl.CostEstimate(
            flops=12 * local_k * local_m * width, bytes_accessed=4 * local_k * (local_m + width), transcendentals=0),
        compiler_params=pltpu.CompilerParams(
            collective_id=0, has_side_effects=True, vmem_limit_bytes=60 * 1024 * 1024),
    )(amplitudes, integrals, pair_irrep, column_irrep)


def solution(mesh):
    placed = (P("row", "groups"), P("row", "groups"), P("groups"), P("groups"))
    return jax.shard_map(
        functools.partial(shards, mesh.shape["row"]), mesh=mesh, in_specs=placed, out_specs=P("row", "groups"),
        check_vma=False)
```

```python
import functools

import jax
import jax.numpy as jnp
from jax import lax
from jax.experimental import pallas as pl
from jax.experimental.pallas import tpu as pltpu
from jax.sharding import PartitionSpec as P

TILE = 64
MESH = pl.DeviceIdType.MESH
BOUNDS = (11, 20, 32, 44, 56, 64)
CHUNKS = len(BOUNDS) - 1
OWN_AT = 3


def split(x):
    high = x.astype(jnp.bfloat16)
    low = (x - high.astype(jnp.float32)).astype(jnp.bfloat16)
    return high, low


def kernel(depth, a_hbm, b_hbm, pair_ref, column_ref, out_ref, a_buf, b_buf, b_high, b_low, part, from_y, from_z, early_z, early_y,
           a_cross, cross_out, cross_in,
           a_sem, b_sem, a_send, a_recv, b_send, b_recv, y_send, y_recv, z_send, z_recv, ez_send, ez_recv, ey_send, ey_recv,
           ac_sem, c_send, c_recv):
    local_k, width = b_hbm.shape
    rows = out_ref.shape[0]
    bounds = [rows * bound // 64 for bound in BOUNDS]
    spans = [pl.ds(start, end - start) for start, end in zip(bounds, bounds[1:])]
    head = pl.ds(0, bounds[0])
    half = rows // 2
    last = depth - 1
    me = lax.axis_index("row")
    z, y, c = me // 4, (me // 2) % 2, me % 2
    sibling = me + 1 - 2 * c
    across = me + 2 - 4 * y
    up, down = z < depth - 1, z > 0

    order = []
    low, high = z * 0, z * 0 + depth - 1
    for _ in range(depth):
        take_high = (high - z) > (z - low)
        order.append(jnp.where(take_high, high, low))
        low, high = jnp.where(take_high, low, low + 1), jnp.where(take_high, high - 1, high)

    def layer(s):
        found = order[0]
        for k in range(1, depth):
            found = jnp.where(s == k, order[k], found)
        return found

    def columns(b, core, t):
        other = 1 - b // depth
        side = y + other * (1 - 2 * y)
        owner = 4 * layer(b % depth) + 2 * side + core
        return pl.ds(pl.multiple_of(owner * rows + t * half, half), half)

    def slot_of(step):
        moved = jnp.where(step < OWN_AT, step, jnp.where(step == OWN_AT, last, step - 1))
        return jnp.where(step < depth, moved, step)

    def a_local(b, t):
        return pltpu.make_async_copy(
            a_hbm.at[:, columns(b, c, t)], a_buf.at[b, t, pl.ds(0, local_k)], a_sem.at[b, t])

    def a_swap(b, t):
        return pltpu.make_async_remote_copy(
            src_ref=a_hbm.at[:, columns(b, 1 - c, t)], dst_ref=a_buf.at[b, t, pl.ds(local_k, local_k)],
            send_sem=a_send.at[b, t], recv_sem=a_recv.at[b, t], device_id={"row": sibling}, device_id_type=MESH)

    pieces = [(start, end) for start, end in zip([0] + bounds, bounds) if end <= half]
    a_other = pltpu.make_async_copy(a_hbm.at[:, columns(0, 1 - c, 0)], a_cross, ac_sem)

    def cross(p):
        start, end = pieces[p]
        span = pl.ds(start, end - start)
        return pltpu.make_async_remote_copy(
            src_ref=cross_out.at[span], dst_ref=cross_in.at[span], send_sem=c_send.at[p], recv_sem=c_recv.at[p],
            device_id={"row": sibling}, device_id_type=MESH)

    b_local = pltpu.make_async_copy(b_hbm, b_buf.at[pl.ds(0, local_k)], b_sem)
    b_swap = pltpu.make_async_remote_copy(
        src_ref=b_hbm, dst_ref=b_buf.at[pl.ds(local_k, local_k)], send_sem=b_send, recv_sem=b_recv,
        device_id={"row": sibling}, device_id_type=MESH)

    def y_copy(s, q):
        span = spans[q]
        return pltpu.make_async_remote_copy(
            src_ref=part.at[s, span], dst_ref=from_y.at[s, span], send_sem=y_send.at[s, q], recv_sem=y_recv.at[s, q],
            device_id={"row": across}, device_id_type=MESH)

    def z_copy(s, q):
        target = layer(s)
        step = jnp.where(target > z, 1, -1)
        slot = landing(target)
        span = spans[q]
        return pltpu.make_async_remote_copy(
            src_ref=part.at[depth + s, span], dst_ref=from_z.at[slot, span], send_sem=z_send.at[s, q],
            recv_sem=z_recv.at[slot, q], device_id={"row": me + 4 * step}, device_id_type=MESH)

    def landing(target):
        arrives_from_above = (target < z) & (z - 1 == target)
        return jnp.where(arrives_from_above, depth, target)

    def early_z_copy(side, s):
        target = layer(s)
        step = jnp.where(target > z, 1, -1)
        slot = side * (depth + 1) + landing(target)
        return pltpu.make_async_remote_copy(
            src_ref=part.at[side * depth + s, head], dst_ref=early_z.at[slot], send_sem=ez_send.at[side * depth + s],
            recv_sem=ez_recv.at[slot], device_id={"row": me + 4 * step}, device_id_type=MESH)

    def early_z_arrival(slot):
        return pltpu.make_async_remote_copy(
            src_ref=early_z.at[slot], dst_ref=early_z.at[slot], send_sem=ez_send.at[0],
            recv_sem=ez_recv.at[slot], device_id={"row": across}, device_id_type=MESH)

    early_y_copy = pltpu.make_async_remote_copy(
        src_ref=part.at[last, head], dst_ref=early_y, send_sem=ey_send, recv_sem=ey_recv,
        device_id={"row": across}, device_id_type=MESH)

    def z_arrival(slot, q):
        span = spans[q]
        return pltpu.make_async_remote_copy(
            src_ref=from_z.at[slot, span], dst_ref=from_z.at[slot, span], send_sem=z_send.at[0, q],
            recv_sem=z_recv.at[slot, q], device_id={"row": across}, device_id_type=MESH)

    barrier = pltpu.get_barrier_semaphore()
    pl.semaphore_signal(barrier, inc=1, device_id={"row": sibling}, device_id_type=MESH)
    pl.semaphore_signal(barrier, inc=1, device_id={"row": across}, device_id_type=MESH)

    @pl.when(up)
    def _():
        pl.semaphore_signal(barrier, inc=1, device_id={"row": me + 4}, device_id_type=MESH)

    @pl.when(down)
    def _():
        pl.semaphore_signal(barrier, inc=1, device_id={"row": me - 4}, device_id_type=MESH)

    b_local.start()
    a_other.start()
    a_local(0, 0).start()
    a_local(0, 1).start()
    block_of = lax.broadcasted_iota(jnp.int32, (TILE, width), 1) // TILE
    labels = jnp.zeros((TILE, width), jnp.int32)
    for j in range(width // TILE):
        labels = jnp.where(block_of == j, column_ref[j], labels)

    def mask(i, owner, base):
        span = pl.ds(pl.multiple_of(base + i * TILE, TILE), TILE)
        label = pair_ref[owner * (local_k // TILE) + i]
        kept = jnp.where(labels == label, b_buf[span, :], 0.0)
        b_high[span, :], b_low[span, :] = split(kept)

    b_local.wait()
    for i in range(local_k // TILE):
        mask(i, me, 0)
    def product(x, span):
        high, low = split(x.T)
        dot = functools.partial(jnp.dot, preferred_element_type=jnp.float32)
        return dot(high, b_high[span, :]) + dot(high, b_low[span, :]) + dot(low, b_high[span, :])

    own, both = pl.ds(0, local_k), pl.ds(0, 2 * local_k)
    a_other.wait()
    cross_out[...] = product(a_cross[...], own)

    pl.semaphore_wait(barrier, 2 + jnp.where(up, 1, 0) + jnp.where(down, 1, 0))

    for p in range(len(pieces)):
        cross(p).start()
    b_swap.start()
    a_swap(0, 1).start()
    for step in range(1, 2 * depth):
        for t in range(2):
            a_local(slot_of(step), t).start()

    def is_fed(s):
        target = layer(s)
        return ((target > z) & down) | ((target < z) & up)

    a_local(0, 0).wait()
    part[0, pl.ds(0, half), :] = product(a_buf[0, 0, own, :], own)
    for p, (start, end) in enumerate(pieces):
        span = pl.ds(start, end - start)
        cross(p).wait_recv()
        part[0, span, :] += cross_in[span, :]
        if p == 0:
            @pl.when(jnp.logical_not(is_fed(0)))
            def _():
                early_z_copy(0, 0).start()
        else:
            y_copy(0, p - 1).start()

    b_swap.wait_recv()
    for i in range(local_k // TILE):
        mask(i, sibling, local_k)

    def tile(step, b, t):
        side, s = b // depth, b % depth
        a_local(b, t).wait()
        a_swap(b, t).wait_recv()
        part[b, pl.ds(t * half, half), :] = product(a_buf[b, t], both)

        if t == 0:
            @pl.when((s < last) & jnp.logical_not(is_fed(s)))
            def _():
                early_z_copy(side, s).start()

        @pl.when(step < depth)
        def _():
            for q in range(CHUNKS):
                if half * t < bounds[q + 1] <= half * (t + 1):
                    y_copy(b, q).start()

    def swap_next(step):
        for t in range(2):
            a_swap(slot_of(step + 1), t).start()

    def multiply(step, _):
        @pl.when(step < 2 * depth - 1)
        def _():
            swap_next(step)

        for t in range(2):
            tile(step, slot_of(step), t)
        return 0

    swap_next(0)
    tile(0, 0, 1)
    lax.fori_loop(1, 2 * depth, multiply, 0)

    def early_forward(s, _):
        @pl.when(is_fed(s))
        def _():
            for side in range(2):
                slot = side * (depth + 1) + layer(s)
                early_z_arrival(slot).wait_recv()
                part[side * depth + s, head, :] += early_z[slot]
                early_z_copy(side, s).start()
        return 0

    lax.fori_loop(0, last, early_forward, 0)

    def forward(s, _):
        fed = is_fed(s)
        target = layer(s)
        for q in range(CHUNKS):
            span = spans[q]
            y_copy(s, q).wait_recv()
            part[depth + s, span, :] += from_y[s, span, :]

            @pl.when(fed)
            def _():
                z_arrival(target, q).wait_recv()
                part[depth + s, span, :] += from_z[target, span, :]

            z_copy(s, q).start()
        return 0

    lax.fori_loop(0, 2, forward, 0)

    for side in range(2):
        @pl.when(down)
        def _():
            slot = side * (depth + 1) + z
            early_z_arrival(slot).wait_recv()
            part[side * depth + last, head, :] += early_z[slot]

        @pl.when(up)
        def _():
            slot = side * (depth + 1) + depth
            early_z_arrival(slot).wait_recv()
            part[side * depth + last, head, :] += early_z[slot]

        if side == 0:
            early_y_copy.start()

    lax.fori_loop(2, last, forward, 0)

    for q in range(CHUNKS):
        span = spans[q]
        y_copy(last, q).wait_recv()
        out_ref[span, :] = part[depth + last, span, :] + from_y[last, span, :]

        @pl.when(down)
        def _():
            z_arrival(z, q).wait_recv()
            out_ref[span, :] += from_z[z, span, :]

        @pl.when(up)
        def _():
            z_arrival(depth, q).wait_recv()
            out_ref[span, :] += from_z[depth, span, :]

    early_y_copy.wait_recv()
    out_ref[head, :] = part[depth + last, head, :] + early_y[...]
    early_y_copy.wait_send()
    for p in range(len(pieces)):
        cross(p).wait_send()
    b_swap.wait_send()

    def finish(s, _):
        @pl.when(s > 0)
        def _():
            a_swap(s, 0).wait_send()

        a_swap(s, 1).wait_send()
        for t in range(2):
            a_swap(depth + s, t).wait_send()
        for q in range(CHUNKS):
            y_copy(s, q).wait_send()

            @pl.when(s < last)
            def _():
                z_copy(s, q).wait_send()

        @pl.when(s < last)
        def _():
            early_z_copy(0, s).wait_send()
            early_z_copy(1, s).wait_send()
        return 0

    lax.fori_loop(0, depth, finish, 0)


def shards(devices, amplitudes, integrals, pair_irrep, column_irrep):
    depth = devices // 4
    local_k, local_m = amplitudes.shape
    width = integrals.shape[1]
    rows = local_m // devices
    early = rows * BOUNDS[0] // 64
    scratch = [
        pltpu.VMEM((2 * depth, 2, 2 * local_k, rows // 2), jnp.float32),
        pltpu.VMEM((2 * local_k, width), jnp.float32),
        pltpu.VMEM((2 * local_k, width), jnp.bfloat16),
        pltpu.VMEM((2 * local_k, width), jnp.bfloat16),
        pltpu.VMEM((2 * depth, rows, width), jnp.float32),
        pltpu.VMEM((depth, rows, width), jnp.float32),
        pltpu.VMEM((depth + 1, rows, width), jnp.float32),
        pltpu.VMEM((2 * (depth + 1), early, width), jnp.float32),
        pltpu.VMEM((early, width), jnp.float32),
        pltpu.VMEM((local_k, rows // 2), jnp.float32),
        pltpu.VMEM((rows // 2, width), jnp.float32),
        pltpu.VMEM((rows // 2, width), jnp.float32),
        pltpu.SemaphoreType.DMA((2 * depth, 2)),
        pltpu.SemaphoreType.DMA,
        pltpu.SemaphoreType.DMA((2 * depth, 2)),
        pltpu.SemaphoreType.DMA((2 * depth, 2)),
        pltpu.SemaphoreType.DMA,
        pltpu.SemaphoreType.DMA,
        pltpu.SemaphoreType.DMA((depth, CHUNKS)),
        pltpu.SemaphoreType.DMA((depth, CHUNKS)),
        pltpu.SemaphoreType.DMA((depth, CHUNKS)),
        pltpu.SemaphoreType.DMA((depth + 1, CHUNKS)),
        pltpu.SemaphoreType.DMA((2 * depth,)),
        pltpu.SemaphoreType.DMA((2 * (depth + 1),)),
        pltpu.SemaphoreType.DMA,
        pltpu.SemaphoreType.DMA,
        pltpu.SemaphoreType.DMA,
        pltpu.SemaphoreType.DMA((CHUNKS,)),
        pltpu.SemaphoreType.DMA((CHUNKS,)),
    ]
    return pl.pallas_call(
        functools.partial(kernel, depth),
        out_shape=pltpu.VMEM((rows, width), jnp.float32),
        in_specs=[
            pl.BlockSpec(memory_space=pl.ANY),
            pl.BlockSpec(memory_space=pl.ANY),
            pl.BlockSpec(memory_space=pltpu.SMEM),
            pl.BlockSpec(memory_space=pltpu.SMEM),
        ],
        out_specs=pl.BlockSpec(memory_space=pltpu.VMEM),
        scratch_shapes=scratch,
        cost_estimate=pl.CostEstimate(
            flops=12 * local_k * local_m * width, bytes_accessed=4 * local_k * (local_m + width), transcendentals=0),
        compiler_params=pltpu.CompilerParams(
            collective_id=0, has_side_effects=True, vmem_limit_bytes=60 * 1024 * 1024),
    )(amplitudes, integrals, pair_irrep, column_irrep)


def solution(mesh):
    placed = (P("row", "groups"), P("row", "groups"), P("groups"), P("groups"))
    return jax.shard_map(
        functools.partial(shards, mesh.shape["row"]), mesh=mesh, in_specs=placed, out_specs=P("row", "groups"),
        check_vma=False)
```
